32 devices in a mesh: fsdp: 8 (over z, x), tp: 4 (over y, core).
Axes of the slice: x: 2, y: 2, z: 4, core: 2. Of those that a mesh axis runs over, the one named last changes fastest.
Arguments:
- hidden: bfloat16 [2048, 14336], P('fsdp', 'tp'), may hold values from -6 to 6
- cotangent: bfloat16 [2048, 5120], P('fsdp'), may hold values from -6 to 6
- weight: bfloat16 [14336, 5120], P('tp', 'fsdp'), may hold values from -0.046875 to 0.046875
- prompt_hidden: bfloat16 [1024, 14336], P('fsdp', 'tp'), may hold values from -6 to 6
Outputs:
- grad_hidden: bfloat16 [2048, 14336], P('fsdp', 'tp')
- new_weight: bfloat16 [14336, 5120], P('tp', 'fsdp')
- prompt_out: bfloat16 [1024, 5120], P('fsdp')
The draws below stay inside these ranges and needn't reach their ends.
All inputs are finite; a program needn't handle non-finite values.
Results may differ from the reference program's by a relative error of at most 0.014.
Values may be sent and summed in bfloat16 or wider, within the bound.
A program may use at most 192 MiB of HBM per device.

```python
import math
import jax
import jax.numpy as jnp
from jax import lax

D = 5120
FH = 14336
TOK_DEV = 256
TOKENS = 2048
PROMPTS = 1024
N_FSDP = 8
N_TP = 4


def level_of(rng, dims, split, least, high):
    def one(axis_at, shards_of):
        draws = jax.random.uniform(jax.random.fold_in(jax.random.fold_in(rng, 6), axis_at), (shards_of,), jnp.float32, least / len(split), high / len(split))
        return jnp.repeat(jnp.exp(draws), dims[axis_at] // shards_of).reshape((-1,) + (1,) * (len(dims) - axis_at - 1))

    gain = one(*split[0])
    for cut in split[1:]:
        gain = gain * one(*cut)
    return gain


def centred(key, shape, width, most, split=(), kind=jnp.bfloat16):
    values = width * jax.random.normal(key, shape, jnp.float32)
    if split:
        values = values * level_of(key, shape, split, -0.22, 0.18)
    return jnp.clip(values, -most, most).astype(kind)


def setup_inputs(seed: int = 0) -> dict:
    streams_of = jax.random.split(jax.random.key(seed), 5)
    hidden = centred(streams_of[0], (TOKENS, FH), 1.0, 6.0, ((0, 8), (1, 4)))
    cotangent = centred(streams_of[1], (TOKENS, D), 1.0, 6.0, ((0, 8),))
    weight = centred(streams_of[2], (FH, D), FH ** -0.5, 0.046875, ((0, 4), (1, 8)))
    prompt_hidden = centred(streams_of[3], (PROMPTS, FH), 1.0, 6.0, ((0, 8), (1, 4)))
    return {"hidden": hidden, "cotangent": cotangent, "weight": weight, "prompt_hidden": prompt_hidden}


def reference(hidden, cotangent, weight, prompt_hidden):
    grouped_hidden = hidden.reshape(N_FSDP, TOK_DEV, FH)
    grouped_cot = cotangent.reshape(N_FSDP, TOK_DEV, D)

    def add_group(total, pair):
        part = lax.dot_general(pair[0], pair[1], (((0,), (0,)), ((), ())), preferred_element_type=jnp.float32)
        rounded = lax.optimization_barrier(part.astype(jnp.bfloat16))
        return (total + rounded.astype(jnp.float32), None)
    grad_weight, _ = lax.scan(add_group, jnp.zeros((FH, D), jnp.float32), (grouped_hidden, grouped_cot))
    grad_hidden = lax.dot_general(cotangent, weight, (((1,), (1,)), ((), ())), preferred_element_type=jnp.float32).astype(jnp.bfloat16)
    factor = 0.5 / math.sqrt(TOKENS * FH)
    new_weight = (weight.astype(jnp.float32) - factor * grad_weight).astype(jnp.bfloat16)
    unit_width = FH // N_TP
    prompt_groups = prompt_hidden.reshape(PROMPTS, N_TP, unit_width).transpose(1, 0, 2)
    weight_groups = new_weight.reshape(N_TP, unit_width, D)

    def add_share(total, pair):
        share = jnp.dot(pair[0], pair[1], preferred_element_type=jnp.float32)
        rounded = lax.optimization_barrier(share.astype(jnp.bfloat16))
        return (total + rounded.astype(jnp.float32), None)
    summed, _ = lax.scan(add_share, jnp.zeros((PROMPTS, D), jnp.float32), (prompt_groups, weight_groups))
    prompt_out = summed.astype(jnp.bfloat16)
    return (grad_hidden, new_weight, prompt_out)
```

```python
import math

import jax
import jax.numpy as jnp
from jax import lax
from jax.sharding import PartitionSpec as P

F32, BF16 = jnp.float32, jnp.bfloat16


def block_of(blocks, index):
    return lax.dynamic_index_in_dim(blocks, index, 0, keepdims=False)


def swap_blocks(blocks, axis, stride=1):
    count = lax.axis_size(axis)
    groups = count // stride
    me = lax.axis_index(axis) // stride
    got = [block_of(blocks, me)]
    for k in range(1, groups):
        perm = [(i, (i + k * stride) % count) for i in range(count)]
        got.append(lax.ppermute(block_of(blocks, (me + k) % groups), axis, perm))
    return got


def in_order(items, index):
    count = len(items)
    twice = jnp.stack(items[::-1] * 2)
    return lax.dynamic_slice_in_dim(twice, (count - 1 - index) % count, count, 0)


def gather_by_permutes(block, axis):
    count = lax.axis_size(axis)
    items = [block]
    for k in range(1, count):
        items.append(lax.ppermute(block, axis, [(i, (i + k) % count) for i in range(count)]))
    return in_order(items, lax.axis_index(axis))


def line_gather(block, line, step_of):
    length, at = line
    up, down = [block], [block]
    for k in range(1, length):
        up.append(lax.ppermute(up[-1], "fsdp", step_of(range(k - 1, length - 1), 1)))
        down.append(lax.ppermute(down[-1], "fsdp", step_of(range(1, length - k + 1), -1)))
    return [block] + [
        jnp.where(at >= k, up[k], down[length - k]) for k in range(1, length)
    ]


def body(hidden, cotangent, weight, prompt_hidden):
    tokens, units = hidden.shape
    width = weight.shape[1]
    prompts = prompt_hidden.shape[0]
    n_fsdp, n_tp = lax.axis_size("fsdp"), lax.axis_size("tp")
    length = n_fsdp // 2
    me = lax.axis_index("fsdp")
    tp = lax.axis_index("tp")
    z, x = me // 2, me % 2
    factor = 0.5 / math.sqrt(tokens * n_fsdp * units * n_tp)
    across = [(i, i ^ 1) for i in range(n_fsdp)]

    def step_of(froms, by):
        return [(2 * a + b, 2 * (a + by) + b) for a in froms for b in range(2)]

    part = tokens // n_tp
    rows = lax.dynamic_slice_in_dim(cotangent, tp * part, part, 0)
    rows = rows.reshape(part, length, 2 * width).transpose(1, 0, 2)
    mine = jnp.stack(swap_blocks(rows, "fsdp", 2))
    cot = gather_by_permutes(mine, "tp")
    cot = cot.transpose(1, 0, 2, 3).reshape(length, tokens, 2 * width)
    cot_first = cot[:, :, :width]
    cot_second = cot[:, :, width:]
    cot_own = jnp.where(x == 0, cot_first, cot_second)
    cot_peer = jnp.where(x == 0, cot_second, cot_first)

    weight_peer = lax.ppermute(weight, "fsdp", across)
    line_hidden = line_gather(hidden, (length, z), step_of)

    both = jnp.concatenate([weight, weight_peer], axis=1)
    cot_both = jnp.concatenate([cot_own, cot_peer], axis=2)
    terms = [
        lax.dot_general(cot_both[k], both, (((1,), (1,)), ((), ())), preferred_element_type=F32)
        for k in range(length)
    ]
    up = down = None
    for s in range(1, length):
        send_up, send_down = terms[s], terms[length - s]
        if s > 1:
            send_up = send_up + up.astype(F32)
            send_down = send_down + down.astype(F32)
        up = lax.ppermute(send_up.astype(BF16), "fsdp", step_of(range(0, s), 1))
        down = lax.ppermute(
            send_down.astype(BF16), "fsdp", step_of(range(length - s, length), -1)
        )
    grad_hidden = (terms[0] + up.astype(F32) + down.astype(F32)).astype(BF16)

    grouped = jnp.stack(line_hidden)

    def gradient(cots):
        parts = jnp.einsum("gtf,gtd->gfd", grouped, cots, preferred_element_type=F32)
        return jnp.sum(parts.astype(BF16).astype(F32), axis=0)

    other = lax.ppermute(gradient(cot_peer).astype(BF16), "fsdp", across)
    grad_weight = gradient(cot_own) + other.astype(F32)
    new_weight = (weight.astype(F32) - factor * grad_weight).astype(BF16)

    line_prompt = jnp.stack(line_gather(prompt_hidden, (length, z), step_of))
    pair_prompt = lax.ppermute(line_prompt, "fsdp", across)
    all_prompt = jnp.stack([line_prompt, pair_prompt])
    share = lax.dot_general(
        all_prompt.reshape(n_fsdp * prompts, units), new_weight,
        (((1,), (0,)), ((), ())), preferred_element_type=F32,
    ).astype(BF16)
    piece = prompts // n_tp
    share = share.reshape(n_fsdp, n_tp, piece, width).transpose(1, 0, 2, 3)
    shares = swap_blocks(share, "tp")
    summed = sum(s.astype(F32) for s in shares).astype(BF16)
    summed = summed.reshape(2, length, piece, width)
    pieces = []
    for a in range(2):
        for k in range(length):
            if a == k == 0:
                pieces.append(summed[0, 0])
            else:
                perm = [
                    (i, 2 * ((i // 2 - k) % length) + ((i % 2) ^ a)) for i in range(n_fsdp)
                ]
                pieces.append(lax.ppermute(summed[a, k], "fsdp", perm))
    columns = jnp.stack(pieces).reshape(2, length, piece, width)
    columns = jnp.where(x == 0, columns, columns[::-1])
    columns = jnp.concatenate([columns, columns], axis=1)
    columns = lax.dynamic_slice_in_dim(columns, (length - z) % length, length, 1)
    out_rows = columns.transpose(2, 1, 0, 3).reshape(piece, n_fsdp * width)
    prompt_out = gather_by_permutes(out_rows, "tp").reshape(prompts, n_fsdp * width)
    return (grad_hidden, new_weight, prompt_out)


def solution(mesh):
    placed = (P("fsdp", "tp"), P("fsdp", None), P("tp", "fsdp"), P("fsdp", "tp"))
    return jax.shard_map(
        body,
        mesh=mesh,
        in_specs=placed,
        out_specs=(P("fsdp", "tp"), P("tp", "fsdp"), P("fsdp", None)),
        check_vma=False,
    )
```

```python
import functools
import math

import jax
import jax.numpy as jnp
from jax import lax
from jax.experimental import pallas as pl
from jax.experimental.pallas import tpu as pltpu
from jax.sharding import PartitionSpec as P

F32, BF16 = jnp.float32, jnp.bfloat16


def block_of(blocks, index):
    return lax.dynamic_index_in_dim(blocks, index, 0, keepdims=False)


def swap_blocks(blocks, axis, stride=1):
    count = lax.axis_size(axis)
    groups = count // stride
    me = lax.axis_index(axis) // stride
    got = [block_of(blocks, me)]
    for k in range(1, groups):
        perm = [(i, (i + k * stride) % count) for i in range(count)]
        got.append(lax.ppermute(block_of(blocks, (me + k) % groups), axis, perm))
    return got


def in_order(items, index):
    count = len(items)
    twice = jnp.stack(items[::-1] * 2)
    return lax.dynamic_slice_in_dim(twice, (count - 1 - index) % count, count, 0)


def gather_by_permutes(block, axis):
    count = lax.axis_size(axis)
    items = [block]
    for k in range(1, count):
        items.append(lax.ppermute(block, axis, [(i, (i + k) % count) for i in range(count)]))
    return in_order(items, lax.axis_index(axis))


def line_gather(block, line, step_of):
    length, at = line
    up, down = [block], [block]
    for k in range(1, length):
        up.append(lax.ppermute(up[-1], "fsdp", step_of(range(k - 1, length - 1), 1)))
        down.append(lax.ppermute(down[-1], "fsdp", step_of(range(1, length - k + 1), -1)))
    return [block] + [
        jnp.where(at >= k, up[k], down[length - k]) for k in range(1, length)
    ]


def opening_kernel(n_fsdp, n_tp, hidden, weight, cot, hid, peer, cots,
                   up_send, down_send, hid_recv, w_send, w_recv,
                   line_send, line_recv, tp_send, tp_recv, own):
    length = n_fsdp // 2
    me, tp = lax.axis_index("fsdp"), lax.axis_index("tp")
    z, x = me // 2, me % 2
    part = cot.shape[0] // n_tp
    wide = 2 * weight.shape[1]

    def at_line(index):
        return {"fsdp": 2 * index + x}

    def at_tp(k):
        return {"tp": lax.rem(tp + k, n_tp)}

    pair = {"fsdp": 2 * z + 1 - x}

    def remote(src, dst, send, recv, device):
        return pltpu.make_async_remote_copy(
            src_ref=src, dst_ref=dst, send_sem=send, recv_sem=recv,
            device_id=device, device_id_type=pl.DeviceIdType.MESH,
        )

    barrier = pltpu.get_barrier_semaphore()
    partners = [pair] + [at_line(lax.rem(z + k, length)) for k in range(1, length)]
    partners += [at_tp(k) for k in range(1, n_tp)]
    for device in partners:
        pl.semaphore_signal(
            barrier, inc=1, device_id=device, device_id_type=pl.DeviceIdType.MESH
        )
    pl.semaphore_wait(barrier, len(partners))

    def to_up(source, slot):
        return remote(source, hid.at[slot], up_send.at[slot], hid_recv.at[slot], at_line(z + 1))

    def to_down(source, slot):
        return remote(source, hid.at[slot], down_send.at[slot], hid_recv.at[slot], at_line(z - 1))

    rows = pl.ds(pl.multiple_of(tp * part, part), part)

    def to_line(k):
        other = lax.rem(z + k, length)
        columns = pl.ds(pl.multiple_of(other * wide, wide), wide)
        return remote(
            cot.at[rows, columns], cots.at[tp, z], line_send.at[k], line_recv.at[k],
            at_line(other),
        )

    def to_tp(k):
        return remote(cots.at[tp], cots.at[tp], tp_send.at[k], tp_recv.at[k], at_tp(k))

    for k in range(1, length):
        to_line(k).start()
    pl.when(z < length - 1)(lambda: to_up(hidden, z).start())
    pl.when(z > 0)(lambda: to_down(hidden, z).start())
    weights = remote(weight, peer, w_send, w_recv, pair)
    weights.start()
    keep_hidden = pltpu.make_async_copy(hidden, hid.at[z], own.at[0])
    keep_hidden.start()
    mine = pl.ds(pl.multiple_of(z * wide, wide), wide)
    keep_cot = pltpu.make_async_copy(cot.at[rows, mine], cots.at[tp, z], own.at[1])
    keep_cot.start()

    keep_cot.wait()
    for k in range(1, length):
        source = lax.rem(z + length - k, length)
        remote(
            cots.at[tp, source], cots.at[tp, source], line_send.at[k], line_recv.at[k], pair
        ).wait_recv()
    for k in range(1, n_tp):
        to_tp(k).start()

    def arrived(slot):
        remote(hid.at[slot], hid.at[slot], w_send, hid_recv.at[slot], pair).wait_recv()

    for k in range(1, length):
        @pl.when(z >= k)
        def _():
            arrived(z - k)
            pl.when(z < length - 1)(lambda: to_up(hid.at[z - k], z - k).start())

        @pl.when(z + k < length)
        def _():
            arrived(z + k)
            pl.when(z > 0)(lambda: to_down(hid.at[z + k], z + k).start())

    for k in range(1, n_tp):
        source = lax.rem(tp + n_tp - k, n_tp)
        remote(cots.at[source], cots.at[source], tp_send.at[k], tp_recv.at[k], pair).wait_recv()
    for k in range(1, length):
        to_line(k).wait_send()
    for k in range(1, n_tp):
        to_tp(k).wait_send()
    keep_hidden.wait()
    weights.wait()
    for slot in range(length):
        pl.when((z >= slot) & (z < length - 1))(lambda: to_up(hid.at[slot], slot).wait_send())
        pl.when((z <= slot) & (z > 0))(lambda: to_down(hid.at[slot], slot).wait_send())


def opening(hidden, weight, cotangent):
    n_fsdp, n_tp = lax.axis_size("fsdp"), lax.axis_size("tp")
    length = n_fsdp // 2
    tokens, units = hidden.shape
    width = weight.shape[1]
    dma = pltpu.SemaphoreType.DMA
    anywhere = pl.BlockSpec(memory_space=pl.ANY)
    return pl.pallas_call(
        functools.partial(opening_kernel, n_fsdp, n_tp),
        out_shape=[
            jax.ShapeDtypeStruct((length, tokens, units), BF16),
            jax.ShapeDtypeStruct(weight.shape, BF16),
            jax.ShapeDtypeStruct((n_tp, length, tokens // n_tp, 2 * width), BF16),
        ],
        in_specs=[anywhere] * 3,
        out_specs=[anywhere] * 3,
        scratch_shapes=[
            dma((length,)), dma((length,)), dma((length,)), dma, dma,
            dma((length,)), dma((length,)), dma((n_tp,)), dma((n_tp,)), dma((2,)),
        ],
        compiler_params=pltpu.CompilerParams(collective_id=0, has_side_effects=True),
    )(hidden, weight, cotangent)


def body(hidden, cotangent, weight, prompt_hidden):
    tokens, units = hidden.shape
    width = weight.shape[1]
    prompts = prompt_hidden.shape[0]
    n_fsdp, n_tp = lax.axis_size("fsdp"), lax.axis_size("tp")
    length = n_fsdp // 2
    me = lax.axis_index("fsdp")
    tp = lax.axis_index("tp")
    z, x = me // 2, me % 2
    factor = 0.5 / math.sqrt(tokens * n_fsdp * units * n_tp)
    across = [(i, i ^ 1) for i in range(n_fsdp)]

    def step_of(froms, by):
        return [(2 * a + b, 2 * (a + by) + b) for a in froms for b in range(2)]

    grouped, weight_peer, cot = opening(hidden, weight, cotangent)
    cot = cot.transpose(1, 0, 2, 3).reshape(length, tokens, 2 * width)

    both = jnp.where(
        x == 0,
        jnp.concatenate([weight, weight_peer], axis=1),
        jnp.concatenate([weight_peer, weight], axis=1),
    )
    terms = [
        lax.dot_general(
            block_of(cot, (z + length - k) % length), both,
            (((1,), (1,)), ((), ())), preferred_element_type=F32,
        )
        for k in range(length)
    ]
    up = down = None
    for s in range(1, length):
        send_up, send_down = terms[s], terms[length - s]
        if s > 1:
            send_up = send_up + up.astype(F32)
            send_down = send_down + down.astype(F32)
        send_up, send_down = lax.optimization_barrier(
            (send_up.astype(BF16), send_down.astype(BF16))
        )
        if s == 1:
            cot_later, send_up, send_down = lax.optimization_barrier((cot, send_up, send_down))
        up = lax.ppermute(send_up, "fsdp", step_of(range(0, s), 1))
        down = lax.ppermute(send_down, "fsdp", step_of(range(length - s, length), -1))
    grad_hidden = (terms[0] + up.astype(F32) + down.astype(F32)).astype(BF16)

    cot_first, cot_second = cot_later[:, :, :width], cot_later[:, :, width:]
    cot_own = jnp.where(x == 0, cot_first, cot_second)
    cot_peer = jnp.where(x == 0, cot_second, cot_first)

    def gradient(cots):
        parts = jnp.einsum("gtf,gtd->gfd", grouped, cots, preferred_element_type=F32)
        return jnp.sum(parts.astype(BF16).astype(F32), axis=0)

    other = lax.ppermute(gradient(cot_peer).astype(BF16), "fsdp", across)
    grad_weight = gradient(cot_own) + other.astype(F32)
    new_weight = (weight.astype(F32) - factor * grad_weight).astype(BF16)

    prompt_hidden, _ = lax.optimization_barrier((prompt_hidden, cot_later))
    line_prompt = jnp.stack(line_gather(prompt_hidden, (length, z), step_of))
    pair_prompt = lax.ppermute(line_prompt, "fsdp", across)
    all_prompt = jnp.stack([line_prompt, pair_prompt])
    share = lax.dot_general(
        all_prompt.reshape(n_fsdp * prompts, units), new_weight,
        (((1,), (0,)), ((), ())), preferred_element_type=F32,
    ).astype(BF16)
    piece = prompts // n_tp
    share = share.reshape(n_fsdp, n_tp, piece, width).transpose(1, 0, 2, 3)
    shares = swap_blocks(share, "tp")
    summed = sum(s.astype(F32) for s in shares).astype(BF16)
    summed = summed.reshape(2, length, piece, width)
    pieces = []
    for a in range(2):
        for k in range(length):
            if a == k == 0:
                pieces.append(summed[0, 0])
            else:
                perm = [
                    (i, 2 * ((i // 2 - k) % length) + ((i % 2) ^ a)) for i in range(n_fsdp)
                ]
                pieces.append(lax.ppermute(summed[a, k], "fsdp", perm))
    columns = jnp.stack(pieces).reshape(2, length, piece, width)
    columns = jnp.where(x == 0, columns, columns[::-1])
    columns = jnp.concatenate([columns, columns], axis=1)
    columns = lax.dynamic_slice_in_dim(columns, (length - z) % length, length, 1)
    out_rows = columns.transpose(2, 1, 0, 3).reshape(piece, n_fsdp * width)
    prompt_out = gather_by_permutes(out_rows, "tp").reshape(prompts, n_fsdp * width)
    return (grad_hidden, new_weight, prompt_out)


def solution(mesh):
    placed = (P("fsdp", "tp"), P("fsdp", None), P("tp", "fsdp"), P("fsdp", "tp"))
    return jax.shard_map(
        body,
        mesh=mesh,
        in_specs=placed,
        out_specs=(P("fsdp", "tp"), P("tp", "fsdp"), P("fsdp", None)),
        check_vma=False,
    )
```
